512 devices in a mesh: dp: 64 (over x_lo, z, core), tensor: 8 (over y, x_hi).
Axes of the slice: x: 4 (x_hi: 2, x_lo: 2; x = x_hi * 2 + x_lo), y: 4, z: 16, core: 2. Of those that a mesh axis runs over, the one named last changes fastest.
Arguments:
- train_inputs: bfloat16 [65536, 4096], P('dp', 'tensor'), may hold values from -6 to 6
- train_cotangents: bfloat16 [65536, 14336], P('dp', 'tensor')
- val_inputs: bfloat16 [256, 4096], P('dp', 'tensor'), may hold values from -6 to 6
- val_cotangents: bfloat16 [256, 14336], P('dp', 'tensor'), may hold values from -6 to 6
Outputs:
- weights: float32 [65536], P(('dp', 'tensor'))
- look_ahead: bfloat16 [256, 14336], P('dp', 'tensor')
The draws below stay inside these ranges and needn't reach their ends.
All inputs are finite; a program needn't handle non-finite values.
Results may differ from the reference program's by a relative error of at most 0.0049.
Values may be sent and summed in bfloat16 or wider, within the bound.
A program may use at most 64 MiB of HBM per device.

```python
import math
import jax
import jax.numpy as jnp
from jax import lax

D = 4096
FF = 14336
TOKENS = 65536
VAL = 256


def draw_train_cotangents(key, part):
    key = jax.random.fold_in(key, 11)
    first_key, second_key = jax.random.split(key, 2)
    rising = jnp.exp(jnp.arange(TOKENS, dtype=jnp.float32) * (math.log(3.0) / max(TOKENS - 1, 1)))
    spread = jnp.exp(jax.random.uniform(second_key, (TOKENS, 1), jnp.float32, 0.0, math.log(3.4)))
    values = jnp.clip(jax.random.normal(first_key, (TOKENS, FF), jnp.float32), -6.0, 6.0)
    return (values * rising[:, None] * spread).astype(jnp.bfloat16)


def shard_levels(key, shape, cuts, least, high):
    level, own = 1.0, jax.random.fold_in(key, 6)
    for dim, shards_of in cuts:
        draws = jnp.exp(jax.random.uniform(jax.random.fold_in(own, dim), (shards_of,), jnp.float32, least / len(cuts), high / len(cuts)))
        level = level * jnp.repeat(draws, shape[dim] // shards_of).reshape([-1 if axis == dim else 1 for axis in range(len(shape))])
    return level


def centred(own_key, dims, deviation, limit, cuts=(), kind=jnp.bfloat16):
    entries = jax.random.normal(own_key, dims, jnp.float32) * deviation
    if len(cuts) > 0:
        entries = shard_levels(own_key, dims, cuts, -0.22, 0.18) * entries
    return jnp.clip(entries, min=-limit, max=limit).astype(kind)


def setup_inputs(seed: int = 0) -> dict:
    key_list = jax.random.split(jax.random.key(seed), 5)
    train_inputs = centred(key_list[0], (TOKENS, D), 1.0, 6.0, ((0, 64), (1, 8)))
    train_cotangents = draw_train_cotangents(jax.random.fold_in(key_list[4], 71), 0)
    val_inputs = centred(key_list[2], (VAL, D), 1.0, 6.0, ((0, 64), (1, 8)))
    val_cotangents = centred(key_list[3], (VAL, FF), 1.0, 6.0, ((0, 64), (1, 8)))
    return dict(train_inputs=train_inputs, train_cotangents=train_cotangents, val_inputs=val_inputs, val_cotangents=val_cotangents)


def reference(train_inputs, train_cotangents, val_inputs, val_cotangents):
    input_gram = jnp.dot(train_inputs, val_inputs.T, preferred_element_type=jnp.float32)
    cotangent_gram = jnp.dot(train_cotangents, val_cotangents.T, preferred_element_type=jnp.float32)
    scores = lax.optimization_barrier(jnp.sum(input_gram * cotangent_gram, axis=1)) * (1.0 / math.sqrt(D * FF * VAL))
    raw_weights = jax.nn.softplus(-scores)
    token_total = jnp.sum(raw_weights)
    weights = raw_weights * (TOKENS / token_total)
    coef_rows = (input_gram * raw_weights[:, None]).astype(jnp.bfloat16)
    summed = jnp.dot(coef_rows.T, train_cotangents, preferred_element_type=jnp.float32)
    look_ahead = (summed / token_total).astype(jnp.bfloat16)
    return (weights, look_ahead)
```

```python
import functools
import math

import jax
import jax.numpy as jnp
from jax import lax
from jax.experimental import pallas as pl
from jax.experimental.pallas import tpu as pltpu
from jax.sharding import PartitionSpec as P

D = 4096
FF = 14336
TOKENS = 65536
VAL = 256
NZ = 16
BF = jnp.bfloat16
F32 = jnp.float32
NT = (((1,), (1,)), ((), ()))

RS_T = jnp.float32
AG_T = jnp.bfloat16
HALF = 896


def dot(a, b):
    return jnp.dot(a, b, preferred_element_type=F32)


def remote(src, dst, send, recv, device):
    return pltpu.make_async_remote_copy(
        src_ref=src,
        dst_ref=dst,
        send_sem=send,
        recv_sem=recv,
        device_id=device,
        device_id_type=pl.DeviceIdType.MESH,
    )


def one_hot(rows, columns, column_of_row):
    row = lax.broadcasted_iota(jnp.int32, (rows, columns), 0)
    column = lax.broadcasted_iota(jnp.int32, (rows, columns), 1)
    return jnp.where(column == column_of_row(row), 1.0, 0.0).astype(BF)


def kernel(
    vx_ref, vc_ref, x_hbm, c_hbm, weights_ref, look_ref,
    x_ref, c_ref, g_ref, vx_all, vc_all,
    part_s, part_r, own_part, ig, cg, score,
    coef, lp, core_r, s0, z1_s, z1_r, s1, z2_s, z2_r, x_s, x_r, tot_s, tot_r,
    load_sem, zx_ss, zx_rs, zc_ss, zc_rs, f_ss, f_rs,
    rs_ss, rs_rs, ag_ss, ag_rs, sc_ss, sc_rs, lk_ss, lk_rs,
):
    d, t = lax.axis_index("dp"), lax.axis_index("tensor")
    core, z, xlo = d % 2, (d // 2) % NZ, d // (2 * NZ)

    def at(core=core, z=z, xlo=xlo, t=t):
        return ((xlo * NZ + z) * 2 + core, t)

    def fold(z):
        return (z % 4) * 4 + z // 4

    def zed(step):
        return (z + step + NZ) % NZ

    load_x = pltpu.make_async_copy(x_hbm, x_ref, load_sem.at[0])
    load_c = pltpu.make_async_copy(c_hbm, c_ref, load_sem.at[1])
    load_x.start()
    load_c.start()

    barrier = pltpu.get_barrier_semaphore()

    def greet(device):
        pl.semaphore_signal(
            barrier, inc=1, device_id=device, device_id_type=pl.DeviceIdType.MESH
        )

    def greet_z(i, carry):
        greet(at(z=zed(i)))
        return carry

    def greet_t(i, carry):
        greet(at(t=(t + i) % 8))
        return carry

    lax.fori_loop(1, NZ, greet_z, 0)
    lax.fori_loop(1, 8, greet_t, 0)
    greet(at(core=1 - core))
    greet(at(xlo=1 - xlo))

    mine = g_ref.at[core, fold(z), xlo]
    packed_x = jnp.zeros((16, 128), F32)
    for k in range(4):
        pick = one_hot(16, 4, lambda row: row - 4 * k)
        packed_x += dot(pick, vx_ref[:, k * 128 : (k + 1) * 128])
    mine[0:16, :] = packed_x.astype(BF)
    packed_c = jnp.zeros((64, 128), F32)
    for k in range(14):
        pick = one_hot(64, 4, lambda row: row - 4 * k)
        packed_c += dot(pick, vc_ref[:, k * 128 : (k + 1) * 128])
    mine[16:80, :] = packed_c.astype(BF)
    pl.semaphore_wait(barrier, NZ - 1 + 7 + 2)

    def along_z(i, rows, ss, rs, sender):
        ref = g_ref.at[core, fold(sender), xlo, rows, :]
        return remote(ref, ref, ss.at[i], rs.at[i], at(z=zed(i)))

    rows_x, rows_c = pl.ds(0, 16), pl.ds(16, 64)

    def send_x(i, carry):
        along_z(i, rows_x, zx_ss, zx_rs, z).start()
        return carry

    def send_c(i, carry):
        along_z(i, rows_c, zc_ss, zc_rs, z).start()
        return carry

    lax.fori_loop(1, NZ, send_x, 0)
    lax.fori_loop(1, NZ, send_c, 0)

    def forward(rows, k):
        to_x = g_ref.at[core, :, xlo, rows, :]
        from_x = g_ref.at[core, :, 1 - xlo, rows, :]
        other_a = g_ref.at[1 - core, :, xlo, rows, :]
        other_b = g_ref.at[1 - core, :, 1 - xlo, rows, :]
        x_out = remote(to_x, to_x, f_ss.at[k], f_rs.at[k], at(xlo=1 - xlo))
        a_out = remote(to_x, to_x, f_ss.at[k + 1], f_rs.at[k + 1], at(core=1 - core))
        x_in = remote(from_x, from_x, f_ss.at[k], f_rs.at[k], at(xlo=1 - xlo))
        b_out = remote(from_x, from_x, f_ss.at[k + 2], f_rs.at[k + 2], at(core=1 - core))
        a_in = remote(other_a, other_a, f_ss.at[k + 1], f_rs.at[k + 1], at(core=1 - core))
        b_in = remote(other_b, other_b, f_ss.at[k + 2], f_rs.at[k + 2], at(core=1 - core))
        return x_out, a_out, x_in, b_out, a_in, b_in

    def arrive(rows, ss, rs):
        def body(i, carry):
            along_z(i, rows, ss, rs, zed(-i)).wait_recv()
            return carry

        lax.fori_loop(1, NZ, body, 0)

    def left(rows, ss, rs):
        def body(i, carry):
            along_z(i, rows, ss, rs, z).wait_send()
            return carry

        lax.fori_loop(1, NZ, body, 0)

    arrive(rows_x, zx_ss, zx_rs)
    x_out, a_out, x_in, b_out, a_in, b_in = forward(rows_x, 0)
    x_out.start()
    a_out.start()
    x_in.wait_recv()
    b_out.start()
    a_in.wait_recv()
    b_in.wait_recv()

    order_x = one_hot(64, 64, lambda o: ((o // 4) % 4) * 16 + (o // 16) * 4 + o % 4)

    def lay_x(i, carry):
        block = g_ref[i // 8, pl.ds((i % 8) * 2, 2), :, 0:16, :].reshape(64, 128)
        rows = dot(order_x, block).astype(BF)
        for k in range(4):
            vx_all[pl.ds(pl.multiple_of(i * 16, 16), 16), k * 128 : (k + 1) * 128] = rows[
                k * 16 : (k + 1) * 16
            ]
        return carry

    lax.fori_loop(0, 16, lay_x, 0)
    load_x.wait()

    def owner(i, sender, receiver):
        return remote(
            part_s.at[receiver], part_r.at[sender], rs_ss.at[i], rs_rs.at[i], at(t=receiver)
        )

    def input_part(who):
        block = x_ref[pl.ds(pl.multiple_of(who * 128, 128), 128), :]
        return lax.dot_general(vx_all[...], block, NT, preferred_element_type=F32)

    def send_part(i, carry):
        who = (t + i) % 8
        part_s[who] = input_part(who).astype(RS_T)
        owner(i, t, who).start()
        return carry

    lax.fori_loop(1, 8, send_part, 0)
    own_part[...] = input_part(t)

    arrive(rows_c, zc_ss, zc_rs)
    cx_out, ca_out, cx_in, cb_out, ca_in, cb_in = forward(rows_c, 3)
    cx_out.start()
    ca_out.start()

    def add_part(i, carry):
        sender = (t - i + 8) % 8
        owner(i, sender, t).wait_recv()
        own_part[...] += part_r[sender].astype(F32)
        return carry

    lax.fori_loop(1, 8, add_part, 0)
    ig[t] = own_part[...].astype(AG_T)

    def spread(i, sender):
        return remote(ig.at[sender], ig.at[sender], ag_ss.at[i], ag_rs.at[i], at(t=(t + i) % 8))

    def send_ig(i, carry):
        spread(i, t).start()
        return carry

    lax.fori_loop(1, 8, send_ig, 0)

    cx_in.wait_recv()
    cb_out.start()
    ca_in.wait_recv()
    cb_in.wait_recv()
    order_c = one_hot(224, 256, lambda o: ((o // 4) % 4) * 64 + (o // 16) * 4 + o % 4)

    def lay_c(i, carry):
        block = g_ref[i // 8, pl.ds((i % 8) * 2, 2), :, 16:80, :].reshape(256, 128)
        rows = dot(order_c, block).astype(BF)
        for k in range(14):
            vc_all[pl.ds(pl.multiple_of(i * 16, 16), 16), k * 128 : (k + 1) * 128] = rows[
                k * 16 : (k + 1) * 16
            ]
        return carry

    lax.fori_loop(0, 16, lay_c, 0)
    load_c.wait()

    def cotangent_part(i, carry):
        block = c_ref[pl.ds(pl.multiple_of(i * 256, 256), 256), :]
        part = lax.dot_general(vc_all[...], block, NT, preferred_element_type=F32)
        cg[i * 2] = part[:, :128]
        cg[i * 2 + 1] = part[:, 128:]
        return carry

    lax.fori_loop(0, 4, cotangent_part, 0)

    def take_ig(i, carry):
        spread(i, (t - i + 8) % 8).wait_recv()
        return carry

    lax.fori_loop(1, 8, take_ig, 0)
    rows = [jnp.sum(ig[k].astype(F32) * cg[k], axis=0, keepdims=True) for k in range(8)]
    score[t] = jnp.concatenate(rows, axis=0)

    def share(i, sender):
        return remote(
            score.at[sender], score.at[sender], sc_ss.at[i], sc_rs.at[i], at(t=(t + i) % 8)
        )

    def send_score(i, carry):
        share(i, t).start()
        return carry

    def take_score(i, carry):
        share(i, (t - i + 8) % 8).wait_recv()
        return carry

    lax.fori_loop(1, 8, send_score, 0)
    lax.fori_loop(1, 8, take_score, 0)
    total = score[0]
    for k in range(1, 8):
        total += score[k]
    minus = total * (-1.0 / math.sqrt(D * FF * VAL))
    raw = jnp.maximum(minus, 0.0) + jnp.log1p(jnp.exp(-jnp.abs(minus)))
    for k in range(8):
        coef[:, k * 128 : (k + 1) * 128] = (ig[k].astype(F32) * raw[k : k + 1, :]).astype(BF)
    mine_raw = jnp.sum(
        jnp.where(lax.broadcasted_iota(jnp.int32, (8, 128), 0) == t, raw, 0.0),
        axis=0,
        keepdims=True,
    )
    tot_s[0] = jnp.broadcast_to(jnp.sum(raw, keepdims=True), (8, 128))

    copies = []

    def start(copy):
        copy.start()
        copies.append(copy)
        return copy

    other = pl.ds(pl.multiple_of((1 - core) * 128, 128), 128)
    own = pl.ds(pl.multiple_of(core * 128, 128), 128)

    def cross(n):
        return remote(
            lp.at[n, other, :], core_r.at[n], lk_ss.at[n], lk_rs.at[n], at(core=1 - core)
        )

    tot_core = start(remote(tot_s.at[0], tot_r.at[0], lk_ss.at[7], lk_rs.at[7], at(core=1 - core)))

    def look_part(n, carry):
        lp[n] = dot(coef[...], c_ref[:, pl.ds(pl.multiple_of(n * 256, 256), 256)])
        cross(n).start()
        return carry

    lax.fori_loop(0, 7, look_part, 0)

    def cross_sum(n, carry):
        cross(n).wait_recv()
        part = lp[n, own, :] + core_r[n]
        columns = pl.ds(pl.multiple_of(n * 256, 256), 256)
        for r in range(4):
            rows = part[r * 32 : (r + 1) * 32]
            s0[r, :, columns] = rows
            z1_s[r, :, columns] = rows.astype(BF)
        return carry

    lax.fori_loop(0, 7, cross_sum, 0)
    tot_core.wait_recv()
    tot_s[1] = tot_s[0] + tot_r[0]

    def near(src, dst, k, step):
        return remote(src, dst, lk_ss.at[k], lk_rs.at[k], at(z=zed(step)))

    here = z % 4
    lo, hi = pl.ds(0, HALF), pl.ds(HALF, HALF)
    up2 = start(near(z1_s.at[(here + 2) % 4, :, lo], z1_r.at[2, :, lo], 8, 2))
    down2 = start(near(z1_s.at[(here + 2) % 4, :, hi], z1_r.at[2, :, hi], 9, -2))
    up = start(near(z1_s.at[(here + 1) % 4], z1_r.at[0], 10, 1))
    down = start(near(z1_s.at[(here + 3) % 4], z1_r.at[1], 11, -1))
    tots = [
        start(near(tot_s.at[1], tot_r.at[1 + k], 12 + k, step))
        for k, step in enumerate((1, -1, 2))
    ]
    for copy in (up2, down2, up, down, *tots):
        copy.wait_recv()
    tot_s[2] = tot_s[1] + tot_r[1] + tot_r[2] + tot_r[3]
    total1 = s0[here] + z1_r[0].astype(F32) + z1_r[1].astype(F32) + z1_r[2].astype(F32)
    for q in range(4):
        rows = total1[q * 8 : (q + 1) * 8]
        rows = jnp.concatenate([rows[:, :HALF], rows[:, HALF:]], axis=0)
        s1[q] = rows
        z2_s[q] = rows.astype(z2_s.dtype)

    quarter = z // 4
    far = []
    for k in range(1, 4):
        q = (quarter + k) % 4
        far.append(
            start(remote(z2_s.at[q], z2_r.at[k], lk_ss.at[14 + k], lk_rs.at[14 + k], at(z=zed(4 * k))))
        )
        far.append(
            start(remote(tot_s.at[2], tot_r.at[3 + k], lk_ss.at[17 + k], lk_rs.at[17 + k], at(z=zed(4 * k))))
        )
    for copy in far:
        copy.wait_recv()
    total2 = s1[quarter]
    for k in range(1, 4):
        total2 += z2_r[k].astype(F32)
    x_s[...] = total2
    tot_s[3] = tot_s[2] + tot_r[4] + tot_r[5] + tot_r[6]
    last = start(remote(x_s, x_r, lk_ss.at[21], lk_rs.at[21], at(xlo=1 - xlo)))
    last_tot = start(remote(tot_s.at[3], tot_r.at[7], lk_ss.at[22], lk_rs.at[22], at(xlo=1 - xlo)))
    last.wait_recv()
    last_tot.wait_recv()
    token_total = tot_s[3] + tot_r[7]
    whole = total2 + x_r[...]
    halves = []
    for h in range(2):
        rows = whole[h * 8 : (h + 1) * 8]
        halves.append(jnp.where(xlo == 0, rows[0:4], rows[4:8]))
    out = jnp.concatenate(halves, axis=1) / token_total[0:1, 0:1]
    look_ref[...] = out.astype(BF)
    weights_ref[...] = mine_raw * (TOKENS / token_total[0:1, :])

    left(rows_x, zx_ss, zx_rs)
    left(rows_c, zc_ss, zc_rs)
    for copy in (x_out, a_out, b_out, cx_out, ca_out, cb_out, *copies):
        copy.wait_send()

    def drain_t(i, carry):
        owner(i, t, (t + i) % 8).wait_send()
        spread(i, t).wait_send()
        share(i, t).wait_send()
        return carry

    lax.fori_loop(1, 8, drain_t, 0)

    def drain_core(n, carry):
        cross(n).wait_send()
        return carry

    lax.fori_loop(0, 7, drain_core, 0)


def on_device(train_inputs, train_cotangents, val_inputs, val_cotangents):
    vmem = pl.BlockSpec(memory_space=pltpu.VMEM)
    hbm = pl.BlockSpec(memory_space=pl.ANY)
    dma = pltpu.SemaphoreType.DMA
    weights, look = pl.pallas_call(
        kernel,
        out_shape=(jax.ShapeDtypeStruct((1, 128), F32), jax.ShapeDtypeStruct((4, 1792), BF)),
        in_specs=[vmem, vmem, hbm, hbm],
        out_specs=(vmem, vmem),
        scratch_shapes=[
            pltpu.VMEM((1024, 512), BF),
            pltpu.VMEM((1024, 1792), BF),
            pltpu.VMEM((2, 16, 2, 80, 128), BF),
            pltpu.VMEM((256, 512), BF),
            pltpu.VMEM((256, 1792), BF),
            pltpu.VMEM((8, 256, 128), RS_T),
            pltpu.VMEM((8, 256, 128), RS_T),
            pltpu.VMEM((256, 128), F32),
            pltpu.VMEM((8, 256, 128), AG_T),
            pltpu.VMEM((8, 256, 128), F32),
            pltpu.VMEM((8, 8, 128), F32),
            pltpu.VMEM((256, 1024), BF),
            pltpu.VMEM((7, 256, 256), F32),
            pltpu.VMEM((7, 128, 256), F32),
            pltpu.VMEM((4, 32, 1792), F32),
            pltpu.VMEM((4, 32, 1792), BF),
            pltpu.VMEM((3, 32, 1792), BF),
            pltpu.VMEM((4, 16, HALF), F32),
            pltpu.VMEM((4, 16, HALF), BF),
            pltpu.VMEM((4, 16, HALF), BF),
            pltpu.VMEM((16, HALF), F32),
            pltpu.VMEM((16, HALF), F32),
            pltpu.VMEM((4, 8, 128), F32),
            pltpu.VMEM((8, 8, 128), F32),
            dma((2,)),
            dma((16,)),
            dma((16,)),
            dma((16,)),
            dma((16,)),
            dma((6,)),
            dma((6,)),
            dma((8,)),
            dma((8,)),
            dma((8,)),
            dma((8,)),
            dma((8,)),
            dma((8,)),
            dma((23,)),
            dma((23,)),
        ],
        compiler_params=pltpu.CompilerParams(
            collective_id=0, has_side_effects=True, vmem_limit_bytes=60 << 20
        ),
        name="reweight",
    )(val_inputs, val_cotangents, train_inputs, train_cotangents)
    return weights.reshape(128), look


def solution(mesh):
    return jax.shard_map(
        on_device,
        mesh=mesh,
        in_specs=(P("dp", "tensor"), P("dp", "tensor"), P("dp", "tensor"), P("dp", "tensor")),
        out_specs=(P(("dp", "tensor")), P("dp", "tensor")),
        check_vma=False,
    )
```

```python
import functools
import math

import jax
import jax.numpy as jnp
from jax import lax
from jax.experimental import pallas as pl
from jax.experimental.pallas import tpu as pltpu
from jax.sharding import PartitionSpec as P

D = 4096
FF = 14336
TOKENS = 65536
VAL = 256
NZ = 16
BF = jnp.bfloat16
F32 = jnp.float32
NT = (((1,), (1,)), ((), ()))

HALF = 896
LEFT = 1024
SLOTS = ((0, 12, 1, 13, 2, 14, 15, 3), (4, 8, 5, 9, 6, 10, 7, 11))
SLOT_OF = {o: (h, e) for h in range(2) for e, o in enumerate(SLOTS[h])}
BLOCKS = (0, 12, 4, 8)


def dot(a, b):
    return jnp.dot(a, b, preferred_element_type=F32)


def remote(src, dst, send, recv, device):
    return pltpu.make_async_remote_copy(
        src_ref=src,
        dst_ref=dst,
        send_sem=send,
        recv_sem=recv,
        device_id=device,
        device_id_type=pl.DeviceIdType.MESH,
    )


def one_hot(rows, columns, column_of_row):
    row = lax.broadcasted_iota(jnp.int32, (rows, columns), 0)
    column = lax.broadcasted_iota(jnp.int32, (rows, columns), 1)
    return jnp.where(column == column_of_row(row), 1.0, 0.0).astype(BF)


def kernel(
    vx_ref, vc_ref, x_hbm, c_hbm, weights_ref, look_ref,
    v_ref, x_ref, c_ref, g_ref, vx_all, vc_all,
    part_s, part_r, own_part, ig, cg, score,
    coef, lp, core_r, s0, z1_s, z1_r, z2_s, z2_r, tot_s, tot_r,
    load_sem, zx_ss, zx_rs, zc_ss, zc_rs, f_ss, f_rs,
    rs_ss, rs_rs, ag_ss, ag_rs, sc_ss, sc_rs, co_ss, co_rs, lk_ss, lk_rs,
):
    d, t = lax.axis_index("dp"), lax.axis_index("tensor")
    core, z, xlo = d % 2, (d // 2) % NZ, d // (2 * NZ)

    def at(core=core, z=z, xlo=xlo, t=t):
        return ((xlo * NZ + z) * 2 + core, t)

    def zed(step):
        return (z + step + NZ) % NZ

    loads = [
        pltpu.make_async_copy(src, dst, load_sem.at[k])
        for k, (src, dst) in enumerate(
            ((vx_ref, v_ref.at[:, 0:512]), (vc_ref, v_ref.at[:, 512:2304]), (x_hbm, x_ref), (c_hbm, c_ref))
        )
    ]
    for load in loads:
        load.start()

    barrier = pltpu.get_barrier_semaphore()

    def greet(device):
        pl.semaphore_signal(
            barrier, inc=1, device_id=device, device_id_type=pl.DeviceIdType.MESH
        )

    def greet_z(i, carry):
        greet(at(z=zed(i)))
        return carry

    def greet_t(i, carry):
        greet(at(t=(t + i) % 8))
        return carry

    lax.fori_loop(1, NZ, greet_z, 0)
    for step in (-2, 2, -1, 1, 0):
        greet(at(z=zed(step), xlo=1 - xlo))
    lax.fori_loop(1, 8, greet_t, 0)
    greet(at(core=1 - core))

    loads[0].wait()
    loads[1].wait()
    packed_x = jnp.zeros((16, 128), F32)
    for k in range(4):
        pick = one_hot(16, 4, lambda row: row - 4 * k)
        packed_x += dot(pick, v_ref[:, k * 128 : (k + 1) * 128])
    g_ref[0, 0, 0, 0, 0:16, :] = packed_x.astype(BF)
    packed_c = jnp.zeros((64, 128), F32)
    for k in range(14):
        pick = one_hot(64, 4, lambda row: row - 4 * k)
        packed_c += dot(pick, v_ref[:, 512 + k * 128 : 512 + (k + 1) * 128])
    g_ref[0, 0, 0, 0, 16:80, :] = packed_c.astype(BF)
    pl.semaphore_wait(barrier, NZ - 1 + 5 + 7 + 1)

    pending = []

    def start(copy):
        copy.start()
        pending.append(copy)
        return copy

    rows_x, rows_c = pl.ds(0, 16), pl.ds(16, 64)

    def along_z(i, rows, ss, rs):
        h, e = SLOT_OF[NZ - i]
        return remote(
            g_ref.at[0, 0, 0, 0, rows, :], g_ref.at[h, 0, 0, e, rows, :], ss.at[i], rs.at[i], at(z=zed(i))
        )

    near = (4, 13, 3, 14, 2, 15, 1)
    far = (8, 7, 9, 6, 10, 5, 11, 12)
    hops_x = {i: start(along_z(i, rows_x, zx_ss, zx_rs)) for i in near + far}
    hops_c = {i: start(along_z(i, rows_c, zc_ss, zc_rs)) for i in near + far}

    def forward(h, rows, k):
        x_copy = remote(
            g_ref.at[h, 0, 0, :, rows, :], g_ref.at[h, 0, 1, :, rows, :], f_ss.at[k], f_rs.at[k], at(xlo=1 - xlo)
        )
        core_copies = [
            remote(
                g_ref.at[h, 0, a, :, rows, :],
                g_ref.at[h, 1, a, :, rows, :],
                f_ss.at[k + 1 + a],
                f_rs.at[k + 1 + a],
                at(core=1 - core),
            )
            for a in range(2)
        ]
        return x_copy, *core_copies

    fx = [forward(h, rows_x, 3 * h) for h in range(2)]
    fc = [forward(h, rows_c, 6 + 3 * h) for h in range(2)]

    def pass_on(copies, hops, group):
        for i in group:
            hops[i].wait_recv()
        start(copies[0])
        start(copies[1])

    def pass_across(copies):
        copies[0].wait_recv()
        start(copies[2])

    def complete(copies):
        copies[1].wait_recv()
        copies[2].wait_recv()

    order_x = one_hot(64, 64, lambda o: ((o // 4) % 4) * 16 + (o // 16) * 4 + o % 4)
    order_c = one_hot(224, 256, lambda o: ((o // 4) % 4) * 64 + (o // 16) * 4 + o % 4)

    def lay(h, rows, order, out, tiles):
        def body(i, carry):
            block = g_ref[h, i // 4, (i // 2) % 2, pl.ds((i % 2) * 4, 4), rows, :]
            laid = dot(order, block.reshape(order.shape[1], 128)).astype(BF)
            for k in range(tiles):
                out[pl.ds(pl.multiple_of(h * 128 + i * 16, 16), 16), k * 128 : (k + 1) * 128] = laid[
                    k * 16 : (k + 1) * 16
                ]
            return carry

        lax.fori_loop(0, 8, body, 0)

    def owner(h, i, sender, receiver):
        return remote(
            part_s.at[h, receiver], part_r.at[h, sender], rs_ss.at[h, i], rs_rs.at[h, i], at(t=receiver)
        )

    def spread(h, i, sender):
        ref = ig.at[h, sender]
        return remote(ref, ref, ag_ss.at[h, i], ag_rs.at[h, i], at(t=(t + i) % 8))

    def input_part(h, who):
        block = x_ref[pl.ds(pl.multiple_of(who * 128, 128), 128), :]
        return lax.dot_general(
            vx_all[h * 128 : (h + 1) * 128, :], block, NT, preferred_element_type=F32
        )

    def send_parts(h):
        def body(i, carry):
            who = (t + i) % 8
            part_s[h, who] = input_part(h, who).astype(BF)
            owner(h, i, t, who).start()
            return carry

        lax.fori_loop(1, 8, body, 0)
        own_part[h] = input_part(h, t)

    def add_parts(h):
        def body(i, carry):
            sender = (t - i + 8) % 8
            owner(h, i, sender, t).wait_recv()
            own_part[h] += part_r[h, sender].astype(F32)
            return carry

        lax.fori_loop(1, 8, body, 0)
        ig[h, t] = own_part[h].astype(BF)

        def send(i, carry):
            spread(h, i, t).start()
            return carry

        lax.fori_loop(1, 8, send, 0)

    def take_ig(h):
        def body(i, carry):
            spread(h, i, (t - i + 8) % 8).wait_recv()
            return carry

        lax.fori_loop(1, 8, body, 0)

    pass_on(fx[0], hops_x, near)
    pass_across(fx[0])
    pass_on(fx[1], hops_x, far)
    loads[2].wait()
    complete(fx[0])
    lay(0, rows_x, order_x, vx_all, 4)
    send_parts(0)
    pass_across(fx[1])
    complete(fx[1])
    lay(1, rows_x, order_x, vx_all, 4)
    send_parts(1)
    pass_on(fc[0], hops_c, near)
    add_parts(0)
    pass_on(fc[1], hops_c, far)
    pass_across(fc[0])
    add_parts(1)
    pass_across(fc[1])
    complete(fc[0])
    lay(0, rows_c, order_c, vc_all, 14)
    complete(fc[1])
    lay(1, rows_c, order_c, vc_all, 14)
    loads[3].wait()

    def cotangent_part(i, carry):
        block = c_ref[pl.ds(pl.multiple_of(i * 256, 256), 256), :]
        part = lax.dot_general(vc_all[...], block, NT, preferred_element_type=F32)
        cg[i * 2] = part[:, :128]
        cg[i * 2 + 1] = part[:, 128:]
        return carry

    lax.fori_loop(0, 4, cotangent_part, 0)
    terms = []
    for h in range(2):
        take_ig(h)
        terms.append(
            [
                jnp.sum(ig[h, k].astype(F32) * cg[k, h * 128 : (h + 1) * 128], axis=0, keepdims=True)
                for k in range(8)
            ]
        )
    score[t] = jnp.concatenate([a + b for a, b in zip(*terms)], axis=0)

    def share(i, sender):
        return remote(
            score.at[sender], score.at[sender], sc_ss.at[i], sc_rs.at[i], at(t=(t + i) % 8)
        )

    def send_score(i, carry):
        share(i, t).start()
        return carry

    def take_score(i, carry):
        share(i, (t - i + 8) % 8).wait_recv()
        return carry

    lax.fori_loop(1, 8, send_score, 0)
    lax.fori_loop(1, 8, take_score, 0)
    total = score[0]
    for k in range(1, 8):
        total += score[k]
    minus = total * (-1.0 / math.sqrt(D * FF * VAL))
    raw = jnp.maximum(minus, 0.0) + jnp.log1p(jnp.exp(-jnp.abs(minus)))
    for h in range(2):
        for k in range(8):
            exact = ig[h, k].astype(F32) * raw[k : k + 1, :]
            high = exact.astype(BF)
            columns = slice(k * 128, (k + 1) * 128)
            coef[h * 128 : (h + 1) * 128, columns] = high
            coef[256 + h * 128 : 256 + (h + 1) * 128, columns] = (exact - high.astype(F32)).astype(BF)
    mine_raw = jnp.sum(
        jnp.where(lax.broadcasted_iota(jnp.int32, (8, 128), 0) == t, raw, 0.0),
        axis=0,
        keepdims=True,
    )
    tot_s[0] = jnp.broadcast_to(jnp.sum(raw, keepdims=True), (8, 128))

    used = iter(range(64))

    def move(src, dst, device):
        k = next(used)
        return start(remote(src, dst, lk_ss.at[k], lk_rs.at[k], device))

    def cross(n):
        return remote(
            lp.at[n, :, 1], core_r.at[n], co_ss.at[n], co_rs.at[n], at(core=1 - core)
        )

    tot_core = move(tot_s.at[0], tot_r.at[0], at(core=1 - core))

    def look_part(n):
        part = dot(coef[...], c_ref[:, pl.ds(pl.multiple_of(n * 256, 256), 256)])
        lp[n] = (part[:256] + part[256:]).reshape(2, 2, 64, 256)
        cross(n).start()

    def cross_sum(n):
        cross(n).wait_recv()
        part = lp[n, :, 0] + core_r[n]
        columns = pl.ds(pl.multiple_of(n * 256, 256), 256)
        for a in range(2):
            for r in range(4):
                first = (a * 4 + r) * 8
                rows = jnp.concatenate([part[0, first : first + 8], part[1, first : first + 8]], axis=0)
                z1_s[a, r, :, columns] = rows.astype(BF)
                if a == 0 and r == 0:
                    s0[:, columns] = rows

    def send_near(columns, two):
        copies = []
        for a, step, slot in (
            (1, two, 5), (0, two, 6), (1, -1, 3), (1, 1, 1), (0, -1, 4), (0, 1, 2), (1, 0, 0)
        ):
            copies.append(
                move(
                    z1_s.at[a, step % 4, :, columns],
                    z1_r.at[pl.ds(slot * 16, 16), columns],
                    at(z=zed(step), xlo=(xlo + a) % 2),
                )
            )
        return copies

    lo, hi = pl.ds(0, LEFT), pl.ds(LEFT, 1792 - LEFT)

    def both(n, carry):
        look_part(n)
        cross_sum(n - 2)
        return carry

    look_part(0)
    look_part(1)
    lax.fori_loop(2, 6, both, 0)
    near_lo = send_near(lo, 2)
    look_part(6)
    tot_core.wait_recv()
    tot_s[1] = tot_s[0] + tot_r[0]
    tots = []
    for k, (a, step) in enumerate(((1, 2), (0, 2), (1, -1), (1, 1), (0, -1), (0, 1), (1, 0))):
        tots.append(move(tot_s.at[1], tot_r.at[1 + k], at(z=zed(step), xlo=(xlo + a) % 2)))
    for n in range(4, 7):
        cross_sum(n)
    near_hi = send_near(hi, -2)

    def gather_near(back_two):
        row = lax.broadcasted_iota(jnp.int32, (16, 112), 0)
        column = lax.broadcasted_iota(jnp.int32, (16, 112), 1)
        block, slot = row // 4, column // 16
        one = jnp.where(block == 0, 0, jnp.where(block == 1, 3, block - 1))
        two = jnp.where(block == 0, 1, jnp.where(block == 1, 3, jnp.where(block == 2, 0, 2)))
        source = jnp.where((slot == 3) | (slot == 4), one, block)
        if back_two:
            source = jnp.where(slot >= 5, two, source)
        return jnp.where(column % 16 == source * 4 + row % 4, 1.0, 0.0).astype(BF)

    for copy in near_lo:
        copy.wait_recv()
    left_sum = s0[:, :LEFT] + dot(gather_near(False), z1_r[:, :LEFT])
    for copy in near_hi:
        copy.wait_recv()
    right_sum = s0[:, LEFT:] + dot(gather_near(True), z1_r[:, LEFT:])
    sums = jnp.concatenate([left_sum, right_sum], axis=1)
    for b in (3, 1, 2, 0):
        rows = sums[b * 4 : (b + 1) * 4]
        z2_s[b] = jnp.concatenate([rows[:, :HALF], rows[:, HALF:]], axis=0)
    away = [move(z2_s.at[b], z2_r.at[b], at(z=zed(BLOCKS[b]))) for b in (3, 1, 2)]
    total = tot_s[1]
    for k, copy in enumerate(tots):
        copy.wait_recv()
        total += tot_r[1 + k]
    tot_s[2] = total
    for b in (3, 1, 2):
        away.append(move(tot_s.at[2], tot_r.at[7 + b], at(z=zed(BLOCKS[b]))))
    for copy in away:
        copy.wait_recv()
    token_total = tot_s[2] + tot_r[8] + tot_r[9] + tot_r[10]
    whole = z2_s[0] + z2_r[1] + z2_r[2] + z2_r[3]
    out = jnp.concatenate([whole[0:4], whole[4:8]], axis=1) / token_total[0:1, 0:1]
    look_ref[...] = out.astype(BF)
    weights_ref[...] = mine_raw * (TOKENS / token_total[0:1, :])

    for copy in pending:
        copy.wait_send()

    def drain_t(i, carry):
        for h in range(2):
            owner(h, i, t, (t + i) % 8).wait_send()
            spread(h, i, t).wait_send()
        share(i, t).wait_send()
        return carry

    lax.fori_loop(1, 8, drain_t, 0)

    def drain_core(n, carry):
        cross(n).wait_send()
        return carry

    lax.fori_loop(0, 7, drain_core, 0)


def on_device(train_inputs, train_cotangents, val_inputs, val_cotangents):
    vmem = pl.BlockSpec(memory_space=pltpu.VMEM)
    hbm = pl.BlockSpec(memory_space=pl.ANY)
    dma = pltpu.SemaphoreType.DMA
    weights, look = pl.pallas_call(
        kernel,
        out_shape=(jax.ShapeDtypeStruct((1, 128), F32), jax.ShapeDtypeStruct((4, 1792), BF)),
        in_specs=[hbm] * 4,
        out_specs=(vmem, vmem),
        scratch_shapes=[
            pltpu.VMEM((4, 2304), BF),
            pltpu.VMEM((1024, 512), BF),
            pltpu.VMEM((1024, 1792), BF),
            pltpu.VMEM((2, 2, 2, 8, 80, 128), BF),
            pltpu.VMEM((256, 512), BF),
            pltpu.VMEM((256, 1792), BF),
            pltpu.VMEM((2, 8, 128, 128), BF),
            pltpu.VMEM((2, 8, 128, 128), BF),
            pltpu.VMEM((2, 128, 128), F32),
            pltpu.VMEM((2, 8, 128, 128), BF),
            pltpu.VMEM((8, 256, 128), F32),
            pltpu.VMEM((8, 8, 128), F32),
            pltpu.VMEM((512, 1024), BF),
            pltpu.VMEM((7, 2, 2, 64, 256), F32),
            pltpu.VMEM((7, 2, 64, 256), F32),
            pltpu.VMEM((16, 1792), F32),
            pltpu.VMEM((2, 4, 16, 1792), BF),
            pltpu.VMEM((112, 1792), BF),
            pltpu.VMEM((4, 8, HALF), F32),
            pltpu.VMEM((4, 8, HALF), F32),
            pltpu.VMEM((3, 8, 128), F32),
            pltpu.VMEM((11, 8, 128), F32),
            dma((4,)),
            dma((16,)),
            dma((16,)),
            dma((16,)),
            dma((16,)),
            dma((12,)),
            dma((12,)),
            dma((2, 8)),
            dma((2, 8)),
            dma((2, 8)),
            dma((2, 8)),
            dma((8,)),
            dma((8,)),
            dma((7,)),
            dma((7,)),
            dma((64,)),
            dma((64,)),
        ],
        compiler_params=pltpu.CompilerParams(
            collective_id=0, has_side_effects=True, vmem_limit_bytes=60 << 20
        ),
        name="reweight",
    )(val_inputs, val_cotangents, train_inputs, train_cotangents)
    return weights.reshape(128), look


def solution(mesh):
    return jax.shard_map(
        on_device,
        mesh=mesh,
        in_specs=(P("dp", "tensor"), P("dp", "tensor"), P("dp", "tensor"), P("dp", "tensor")),
        out_specs=(P(("dp", "tensor")), P("dp", "tensor")),
        check_vma=False,
    )
```

```python
import functools
import math

import jax
import jax.numpy as jnp
from jax import lax
from jax.experimental import pallas as pl
from jax.experimental.pallas import tpu as pltpu
from jax.sharding import PartitionSpec as P

D = 4096
FF = 14336
TOKENS = 65536
VAL = 256
NZ = 16
BF = jnp.bfloat16
F32 = jnp.float32
NT = (((1,), (1,)), ((), ()))

HALF = 896
LEFT = 1024
SLOTS = ((0, 12, 1, 13, 2, 14, 15, 3), (4, 8, 5, 9, 6, 10, 7, 11))
SLOT_OF = {o: (h, e) for h in range(2) for e, o in enumerate(SLOTS[h])}
BLOCKS = (0, 12, 4, 8)


def dot(a, b):
    return jnp.dot(a, b, preferred_element_type=F32)


def remote(src, dst, send, recv, device):
    return pltpu.make_async_remote_copy(
        src_ref=src,
        dst_ref=dst,
        send_sem=send,
        recv_sem=recv,
        device_id=device,
        device_id_type=pl.DeviceIdType.MESH,
    )


def one_hot(rows, columns, column_of_row):
    row = lax.broadcasted_iota(jnp.int32, (rows, columns), 0)
    column = lax.broadcasted_iota(jnp.int32, (rows, columns), 1)
    return jnp.where(column == column_of_row(row), 1.0, 0.0).astype(BF)


def kernel(
    vx_ref, vc_ref, x_hbm, c_hbm, weights_ref, look_ref,
    v_ref, x_ref, c_ref, g_ref, vx_all, vc_all,
    part_s, part_r, own_part, ig, cg, score,
    coef, lp, core_r, s0, z1_s, z1_r, z2_s, z2_r, tot_s, tot_r,
    load_sem, zx_ss, zx_rs, zc_ss, zc_rs, f_ss, f_rs,
    rs_ss, rs_rs, ag_ss, ag_rs, sc_ss, sc_rs, co_ss, co_rs, lk_ss, lk_rs,
):
    d, t = lax.axis_index("dp"), lax.axis_index("tensor")
    core, z, xlo = d % 2, (d // 2) % NZ, d // (2 * NZ)

    def at(core=core, z=z, xlo=xlo, t=t):
        return ((xlo * NZ + z) * 2 + core, t)

    def zed(step):
        return (z + step + NZ) % NZ

    loads = [
        pltpu.make_async_copy(src, dst, load_sem.at[k])
        for k, (src, dst) in enumerate(
            ((vx_ref, v_ref.at[:, 0:512]), (vc_ref, v_ref.at[:, 512:2304]), (x_hbm, x_ref), (c_hbm, c_ref))
        )
    ]
    for load in loads:
        load.start()

    barrier = pltpu.get_barrier_semaphore()

    def greet(device):
        pl.semaphore_signal(
            barrier, inc=1, device_id=device, device_id_type=pl.DeviceIdType.MESH
        )

    def greet_z(i, carry):
        greet(at(z=zed(i)))
        return carry

    def greet_t(i, carry):
        greet(at(t=(t + i) % 8))
        return carry

    lax.fori_loop(1, NZ, greet_z, 0)
    for step in (-2, 2, -1, 1, 0):
        greet(at(z=zed(step), xlo=1 - xlo))
    lax.fori_loop(1, 8, greet_t, 0)
    greet(at(core=1 - core))

    loads[0].wait()
    loads[1].wait()
    packed_x = jnp.zeros((16, 128), F32)
    for k in range(4):
        pick = one_hot(16, 4, lambda row: row - 4 * k)
        packed_x += dot(pick, v_ref[:, k * 128 : (k + 1) * 128])
    g_ref[0, 0, 0, 0, 0:16, :] = packed_x.astype(BF)
    packed_c = jnp.zeros((64, 128), F32)
    for k in range(14):
        pick = one_hot(64, 4, lambda row: row - 4 * k)
        packed_c += dot(pick, v_ref[:, 512 + k * 128 : 512 + (k + 1) * 128])
    g_ref[0, 0, 0, 0, 16:80, :] = packed_c.astype(BF)
    pl.semaphore_wait(barrier, NZ - 1 + 5 + 7 + 1)

    pending = []

    def start(copy):
        copy.start()
        pending.append(copy)
        return copy

    rows_x, rows_c = pl.ds(0, 16), pl.ds(16, 64)

    def along_z(i, rows, ss, rs):
        h, e = SLOT_OF[NZ - i]
        return remote(
            g_ref.at[0, 0, 0, 0, rows, :], g_ref.at[h, 0, 0, e, rows, :], ss.at[i], rs.at[i], at(z=zed(i))
        )

    near = (4, 13, 3, 14, 2, 15, 1)
    far = (8, 7, 9, 6, 10, 5, 11, 12)
    hops_x = {i: start(along_z(i, rows_x, zx_ss, zx_rs)) for i in near + far}
    hops_c = {i: start(along_z(i, rows_c, zc_ss, zc_rs)) for i in near + far}

    def forward(h, rows, k):
        x_copy = remote(
            g_ref.at[h, 0, 0, :, rows, :], g_ref.at[h, 0, 1, :, rows, :], f_ss.at[k], f_rs.at[k], at(xlo=1 - xlo)
        )
        core_copies = [
            remote(
                g_ref.at[h, 0, a, :, rows, :],
                g_ref.at[h, 1, a, :, rows, :],
                f_ss.at[k + 1 + a],
                f_rs.at[k + 1 + a],
                at(core=1 - core),
            )
            for a in range(2)
        ]
        return x_copy, *core_copies

    fx = [forward(h, rows_x, 3 * h) for h in range(2)]
    fc = [forward(h, rows_c, 6 + 3 * h) for h in range(2)]

    def pass_on(copies, hops, group):
        for i in group:
            hops[i].wait_recv()
        start(copies[0])
        start(copies[1])

    def pass_across(copies):
        copies[0].wait_recv()
        start(copies[2])

    def complete(copies):
        copies[1].wait_recv()
        copies[2].wait_recv()

    order_x = one_hot(64, 64, lambda o: ((o // 4) % 4) * 16 + (o // 16) * 4 + o % 4)
    order_c = one_hot(224, 256, lambda o: ((o // 4) % 4) * 64 + (o // 16) * 4 + o % 4)

    def lay(h, rows, order, out, tiles):
        for i in range(8):
            block = g_ref[h, i // 4, (i // 2) % 2, (i % 2) * 4 : (i % 2) * 4 + 4, rows, :]
            laid = dot(order, block.reshape(order.shape[1], 128)).astype(BF)
            first = h * 128 + i * 16
            for k in range(tiles):
                out[first : first + 16, k * 128 : (k + 1) * 128] = laid[k * 16 : (k + 1) * 16]

    def owner(h, i, sender, receiver):
        return remote(
            part_s.at[h, receiver], part_r.at[h, sender], rs_ss.at[h, i], rs_rs.at[h, i], at(t=receiver)
        )

    def spread(h, i, sender):
        ref = ig.at[h, sender]
        return remote(ref, ref, ag_ss.at[h, i], ag_rs.at[h, i], at(t=(t + i) % 8))

    def input_part(h, who):
        block = x_ref[pl.ds(pl.multiple_of(who * 128, 128), 128), :]
        return lax.dot_general(
            vx_all[h * 128 : (h + 1) * 128, :], block, NT, preferred_element_type=F32
        )

    def send_parts(h):
        for first, last in ((1, 4), (4, 8)):
            for i in range(first, last):
                part_s[h, (t + i) % 8] = input_part(h, (t + i) % 8).astype(BF)
            for i in range(first, last):
                owner(h, i, t, (t + i) % 8).start()
        own_part[h] = input_part(h, t)

    def add_parts(h):
        def body(i, carry):
            sender = (t - i + 8) % 8
            owner(h, i, sender, t).wait_recv()
            own_part[h] += part_r[h, sender].astype(F32)
            return carry

        lax.fori_loop(1, 8, body, 0)
        ig[h, t] = own_part[h].astype(BF)

        def send(i, carry):
            spread(h, i, t).start()
            return carry

        lax.fori_loop(1, 8, send, 0)

    def take_ig(h):
        def body(i, carry):
            spread(h, i, (t - i + 8) % 8).wait_recv()
            return carry

        lax.fori_loop(1, 8, body, 0)

    pass_on(fx[0], hops_x, near)
    pass_across(fx[0])
    pass_on(fx[1], hops_x, far)
    loads[2].wait()
    complete(fx[0])
    lay(0, rows_x, order_x, vx_all, 4)
    send_parts(0)
    pass_across(fx[1])
    complete(fx[1])
    lay(1, rows_x, order_x, vx_all, 4)
    send_parts(1)
    pass_on(fc[0], hops_c, near)
    add_parts(0)
    pass_on(fc[1], hops_c, far)
    pass_across(fc[0])
    add_parts(1)
    pass_across(fc[1])
    complete(fc[0])
    lay(0, rows_c, order_c, vc_all, 14)
    complete(fc[1])
    lay(1, rows_c, order_c, vc_all, 14)
    loads[3].wait()

    def cotangent_part(i, carry):
        block = c_ref[pl.ds(pl.multiple_of(i * 256, 256), 256), :]
        part = lax.dot_general(vc_all[...], block, NT, preferred_element_type=F32)
        cg[i * 2] = part[:, :128]
        cg[i * 2 + 1] = part[:, 128:]
        return carry

    lax.fori_loop(0, 4, cotangent_part, 0)
    terms = []
    for h in range(2):
        take_ig(h)
        terms.append(
            [
                jnp.sum(ig[h, k].astype(F32) * cg[k, h * 128 : (h + 1) * 128], axis=0, keepdims=True)
                for k in range(8)
            ]
        )
    score[t] = jnp.concatenate([a + b for a, b in zip(*terms)], axis=0)

    def share(i, sender):
        return remote(
            score.at[sender], score.at[sender], sc_ss.at[i], sc_rs.at[i], at(t=(t + i) % 8)
        )

    def send_score(i, carry):
        share(i, t).start()
        return carry

    def take_score(i, carry):
        share(i, (t - i + 8) % 8).wait_recv()
        return carry

    lax.fori_loop(1, 8, send_score, 0)
    lax.fori_loop(1, 8, take_score, 0)
    total = score[0]
    for k in range(1, 8):
        total += score[k]
    minus = total * (-1.0 / math.sqrt(D * FF * VAL))
    raw = jnp.maximum(minus, 0.0) + jnp.log1p(jnp.exp(-jnp.abs(minus)))
    for h in range(2):
        for k in range(8):
            exact = ig[h, k].astype(F32) * raw[k : k + 1, :]
            high = exact.astype(BF)
            columns = slice(k * 128, (k + 1) * 128)
            coef[h * 128 : (h + 1) * 128, columns] = high
            coef[256 + h * 128 : 256 + (h + 1) * 128, columns] = (exact - high.astype(F32)).astype(BF)
    mine_raw = jnp.sum(
        jnp.where(lax.broadcasted_iota(jnp.int32, (8, 128), 0) == t, raw, 0.0),
        axis=0,
        keepdims=True,
    )
    tot_s[0] = jnp.broadcast_to(jnp.sum(raw, keepdims=True), (8, 128))

    used = iter(range(64))

    def move(src, dst, device):
        k = next(used)
        return start(remote(src, dst, lk_ss.at[k], lk_rs.at[k], device))

    def cross(n):
        return remote(
            lp.at[n, :, 1], core_r.at[n], co_ss.at[n], co_rs.at[n], at(core=1 - core)
        )

    tot_core = move(tot_s.at[0], tot_r.at[0], at(core=1 - core))

    def look_part(n):
        part = dot(coef[...], c_ref[:, pl.ds(pl.multiple_of(n * 256, 256), 256)])
        lp[n] = (part[:256] + part[256:]).reshape(2, 2, 64, 256)
        cross(n).start()

    def cross_sum(n):
        cross(n).wait_recv()
        part = lp[n, :, 0] + core_r[n]
        columns = pl.ds(pl.multiple_of(n * 256, 256), 256)
        for a in range(2):
            for r in range(4):
                first = (a * 4 + r) * 8
                rows = jnp.concatenate([part[0, first : first + 8], part[1, first : first + 8]], axis=0)
                z1_s[a, r, :, columns] = rows.astype(BF)
                if a == 0 and r == 0:
                    s0[:, columns] = rows

    def send_near(columns, two):
        copies = []
        for a, step, slot in (
            (1, two, 5), (0, two, 6), (1, -1, 3), (1, 1, 1), (0, -1, 4), (0, 1, 2), (1, 0, 0)
        ):
            copies.append(
                move(
                    z1_s.at[a, step % 4, :, columns],
                    z1_r.at[pl.ds(slot * 16, 16), columns],
                    at(z=zed(step), xlo=(xlo + a) % 2),
                )
            )
        return copies

    lo, hi = pl.ds(0, LEFT), pl.ds(LEFT, 1792 - LEFT)

    def both(n, carry):
        look_part(n)
        cross_sum(n - 2)
        return carry

    look_part(0)
    look_part(1)
    lax.fori_loop(2, 6, both, 0)
    near_lo = send_near(lo, 2)
    look_part(6)
    tot_core.wait_recv()
    tot_s[1] = tot_s[0] + tot_r[0]
    tots = []
    for k, (a, step) in enumerate(((1, 2), (0, 2), (1, -1), (1, 1), (0, -1), (0, 1), (1, 0))):
        tots.append(move(tot_s.at[1], tot_r.at[1 + k], at(z=zed(step), xlo=(xlo + a) % 2)))
    for n in range(4, 7):
        cross_sum(n)
    near_hi = send_near(hi, -2)

    def gather_near(back_two):
        row = lax.broadcasted_iota(jnp.int32, (16, 112), 0)
        column = lax.broadcasted_iota(jnp.int32, (16, 112), 1)
        block, slot = row // 4, column // 16
        one = jnp.where(block == 0, 0, jnp.where(block == 1, 3, block - 1))
        two = jnp.where(block == 0, 1, jnp.where(block == 1, 3, jnp.where(block == 2, 0, 2)))
        source = jnp.where((slot == 3) | (slot == 4), one, block)
        if back_two:
            source = jnp.where(slot >= 5, two, source)
        return jnp.where(column % 16 == source * 4 + row % 4, 1.0, 0.0).astype(BF)

    for copy in near_lo:
        copy.wait_recv()
    left_sum = s0[:, :LEFT] + dot(gather_near(False), z1_r[:, :LEFT])
    for copy in near_hi:
        copy.wait_recv()
    right_sum = s0[:, LEFT:] + dot(gather_near(True), z1_r[:, LEFT:])
    sums = jnp.concatenate([left_sum, right_sum], axis=1)
    for b in (3, 1, 2, 0):
        rows = sums[b * 4 : (b + 1) * 4]
        z2_s[b] = jnp.concatenate([rows[:, :HALF], rows[:, HALF:]], axis=0)
    away = [move(z2_s.at[b], z2_r.at[b], at(z=zed(BLOCKS[b]))) for b in (3, 1, 2)]
    total = tot_s[1]
    for k, copy in enumerate(tots):
        copy.wait_recv()
        total += tot_r[1 + k]
    tot_s[2] = total
    for b in (3, 1, 2):
        away.append(move(tot_s.at[2], tot_r.at[7 + b], at(z=zed(BLOCKS[b]))))
    early = len(pending) - 6
    for copy in pending[:early]:
        copy.wait_send()

    def drain_t(i, carry):
        for h in range(2):
            owner(h, i, t, (t + i) % 8).wait_send()
            spread(h, i, t).wait_send()
        share(i, t).wait_send()
        return carry

    lax.fori_loop(1, 8, drain_t, 0)

    def drain_core(n, carry):
        cross(n).wait_send()
        return carry

    lax.fori_loop(0, 7, drain_core, 0)

    for copy in away:
        copy.wait_recv()
    token_total = tot_s[2] + tot_r[8] + tot_r[9] + tot_r[10]
    whole = z2_s[0] + z2_r[1] + z2_r[2] + z2_r[3]
    out = jnp.concatenate([whole[0:4], whole[4:8]], axis=1) / token_total[0:1, 0:1]
    look_ref[...] = out.astype(BF)
    weights_ref[...] = mine_raw * (TOKENS / token_total[0:1, :])
    for copy in pending[early:]:
        copy.wait_send()


def on_device(train_inputs, train_cotangents, val_inputs, val_cotangents):
    vmem = pl.BlockSpec(memory_space=pltpu.VMEM)
    hbm = pl.BlockSpec(memory_space=pl.ANY)
    dma = pltpu.SemaphoreType.DMA
    weights, look = pl.pallas_call(
        kernel,
        out_shape=(jax.ShapeDtypeStruct((1, 128), F32), jax.ShapeDtypeStruct((4, 1792), BF)),
        in_specs=[hbm] * 4,
        out_specs=(vmem, vmem),
        scratch_shapes=[
            pltpu.VMEM((4, 2304), BF),
            pltpu.VMEM((1024, 512), BF),
            pltpu.VMEM((1024, 1792), BF),
            pltpu.VMEM((2, 2, 2, 8, 80, 128), BF),
            pltpu.VMEM((256, 512), BF),
            pltpu.VMEM((256, 1792), BF),
            pltpu.VMEM((2, 8, 128, 128), BF),
            pltpu.VMEM((2, 8, 128, 128), BF),
            pltpu.VMEM((2, 128, 128), F32),
            pltpu.VMEM((2, 8, 128, 128), BF),
            pltpu.VMEM((8, 256, 128), F32),
            pltpu.VMEM((8, 8, 128), F32),
            pltpu.VMEM((512, 1024), BF),
            pltpu.VMEM((7, 2, 2, 64, 256), F32),
            pltpu.VMEM((7, 2, 64, 256), F32),
            pltpu.VMEM((16, 1792), F32),
            pltpu.VMEM((2, 4, 16, 1792), BF),
            pltpu.VMEM((112, 1792), BF),
            pltpu.VMEM((4, 8, HALF), F32),
            pltpu.VMEM((4, 8, HALF), F32),
            pltpu.VMEM((3, 8, 128), F32),
            pltpu.VMEM((11, 8, 128), F32),
            dma((4,)),
            dma((16,)),
            dma((16,)),
            dma((16,)),
            dma((16,)),
            dma((12,)),
            dma((12,)),
            dma((2, 8)),
            dma((2, 8)),
            dma((2, 8)),
            dma((2, 8)),
            dma((8,)),
            dma((8,)),
            dma((7,)),
            dma((7,)),
            dma((64,)),
            dma((64,)),
        ],
        compiler_params=pltpu.CompilerParams(
            collective_id=0, has_side_effects=True, vmem_limit_bytes=60 << 20
        ),
        name="reweight",
    )(val_inputs, val_cotangents, train_inputs, train_cotangents)
    return weights.reshape(128), look


def solution(mesh):
    return jax.shard_map(
        on_device,
        mesh=mesh,
        in_specs=(P("dp", "tensor"), P("dp", "tensor"), P("dp", "tensor"), P("dp", "tensor")),
        out_specs=(P(("dp", "tensor")), P("dp", "tensor")),
        check_vma=False,
    )
```

```python
import functools
import math

import jax
import jax.numpy as jnp
from jax import lax
from jax.experimental import pallas as pl
from jax.experimental.pallas import tpu as pltpu
from jax.sharding import PartitionSpec as P

D = 4096
FF = 14336
TOKENS = 65536
VAL = 256
NZ = 16
BF = jnp.bfloat16
F32 = jnp.float32
NT = (((1,), (1,)), ((), ()))

HALF = 896
LEFT = 1024
SLOTS = ((0, 12, 1, 13, 2, 14, 15, 3), (4, 8, 5, 9, 6, 10, 7, 11))
SLOT_OF = {o: (h, e) for h in range(2) for e, o in enumerate(SLOTS[h])}
BLOCKS = (0, 12, 4, 8)


def dot(a, b):
    return jnp.dot(a, b, preferred_element_type=F32)


def remote(src, dst, send, recv, device):
    return pltpu.make_async_remote_copy(
        src_ref=src,
        dst_ref=dst,
        send_sem=send,
        recv_sem=recv,
        device_id=device,
        device_id_type=pl.DeviceIdType.MESH,
    )


def one_hot(rows, columns, column_of_row):
    row = lax.broadcasted_iota(jnp.int32, (rows, columns), 0)
    column = lax.broadcasted_iota(jnp.int32, (rows, columns), 1)
    return jnp.where(column == column_of_row(row), 1.0, 0.0).astype(BF)


def kernel(
    vx_ref, vc_ref, x_hbm, c_hbm, weights_ref, look_ref,
    v_ref, x_ref, c_ref, g_ref, vx_all, vc_all,
    part_s, part_r, own_part, ig, cg, score,
    coef, lp, core_r, s0, z1_s, z1_r, z2_s, z2_r, tot_s, tot_r,
    load_sem, zx_ss, zx_rs, zc_ss, zc_rs, f_ss, f_rs,
    rs_ss, rs_rs, ag_ss, ag_rs, sc_ss, sc_rs, co_ss, co_rs, lk_ss, lk_rs,
):
    d, t = lax.axis_index("dp"), lax.axis_index("tensor")
    core, z, xlo = d % 2, (d // 2) % NZ, d // (2 * NZ)

    def at(core=core, z=z, xlo=xlo, t=t):
        return ((xlo * NZ + z) * 2 + core, t)

    def zed(step):
        return (z + step + NZ) % NZ

    barrier = pltpu.get_barrier_semaphore()

    def greet(device):
        pl.semaphore_signal(
            barrier, inc=1, device_id=device, device_id_type=pl.DeviceIdType.MESH
        )

    def greet_t(i, carry):
        greet(at(t=(t + i) % 8))
        return carry

    for step in (8, 7, -7, 6, -6, 5, -5, 4, -4, 3, -3, 2, -2, 1, -1):
        greet(at(z=zed(step)))
    for step in (-2, 2, -1, 1, 0):
        greet(at(z=zed(step), xlo=1 - xlo))
    lax.fori_loop(1, 8, greet_t, 0)
    greet(at(core=1 - core))

    loads = [
        pltpu.make_async_copy(src, dst, load_sem.at[k])
        for k, (src, dst) in enumerate(
            ((vx_ref, v_ref.at[:, 0:512]), (vc_ref, v_ref.at[:, 512:2304]), (x_hbm, x_ref), (c_hbm, c_ref))
        )
    ]
    for load in loads:
        load.start()

    loads[0].wait()
    loads[1].wait()
    packed_x = jnp.zeros((16, 128), F32)
    for k in range(4):
        pick = one_hot(16, 4, lambda row: row - 4 * k)
        packed_x += dot(pick, v_ref[:, k * 128 : (k + 1) * 128])
    g_ref[0, 0, 0, 0, 0:16, :] = packed_x.astype(BF)
    packed_c = jnp.zeros((64, 128), F32)
    for k in range(14):
        pick = one_hot(64, 4, lambda row: row - 4 * k)
        packed_c += dot(pick, v_ref[:, 512 + k * 128 : 512 + (k + 1) * 128])
    g_ref[0, 0, 0, 0, 16:80, :] = packed_c.astype(BF)
    pl.semaphore_wait(barrier, NZ - 1 + 5 + 7 + 1)

    pending = []

    def start(copy):
        copy.start()
        pending.append(copy)
        return copy

    rows_x, rows_c = pl.ds(0, 16), pl.ds(16, 64)

    def along_z(i, rows, ss, rs):
        h, e = SLOT_OF[NZ - i]
        return remote(
            g_ref.at[0, 0, 0, 0, rows, :], g_ref.at[h, 0, 0, e, rows, :], ss.at[i], rs.at[i], at(z=zed(i))
        )

    near = (4, 13, 3, 14, 2, 15, 1)
    far = (8, 7, 9, 6, 10, 5, 11, 12)
    hops_x = {i: start(along_z(i, rows_x, zx_ss, zx_rs)) for i in near + far}
    hops_c = {i: start(along_z(i, rows_c, zc_ss, zc_rs)) for i in near + far}

    def forward(h, rows, k):
        x_copy = remote(
            g_ref.at[h, 0, 0, :, rows, :], g_ref.at[h, 0, 1, :, rows, :], f_ss.at[k], f_rs.at[k], at(xlo=1 - xlo)
        )
        core_copies = [
            remote(
                g_ref.at[h, 0, a, :, rows, :],
                g_ref.at[h, 1, a, :, rows, :],
                f_ss.at[k + 1 + a],
                f_rs.at[k + 1 + a],
                at(core=1 - core),
            )
            for a in range(2)
        ]
        return x_copy, *core_copies

    fx = [forward(h, rows_x, 3 * h) for h in range(2)]
    fc = [forward(h, rows_c, 6 + 3 * h) for h in range(2)]

    def pass_on(copies, hops, group):
        for i in group:
            hops[i].wait_recv()
        start(copies[0])
        start(copies[1])

    def pass_across(copies):
        copies[0].wait_recv()
        start(copies[2])

    def complete(copies):
        copies[1].wait_recv()
        copies[2].wait_recv()

    order_x = one_hot(64, 64, lambda o: ((o // 4) % 4) * 16 + (o // 16) * 4 + o % 4)
    order_c = one_hot(224, 256, lambda o: ((o // 4) % 4) * 64 + (o // 16) * 4 + o % 4)

    def lay(h, rows, order, out, tiles):
        for i in range(8):
            block = g_ref[h, i // 4, (i // 2) % 2, (i % 2) * 4 : (i % 2) * 4 + 4, rows, :]
            laid = dot(order, block.reshape(order.shape[1], 128)).astype(BF)
            first = h * 128 + i * 16
            for k in range(tiles):
                out[first : first + 16, k * 128 : (k + 1) * 128] = laid[k * 16 : (k + 1) * 16]

    def owner(h, i, sender, receiver):
        return remote(
            part_s.at[h, receiver], part_r.at[h, sender], rs_ss.at[h, i], rs_rs.at[h, i], at(t=receiver)
        )

    def spread(h, i, sender):
        ref = ig.at[h, sender]
        return remote(ref, ref, ag_ss.at[h, i], ag_rs.at[h, i], at(t=(t + i) % 8))

    def input_part(h, who):
        block = x_ref[pl.ds(pl.multiple_of(who * 128, 128), 128), :]
        return lax.dot_general(
            vx_all[h * 128 : (h + 1) * 128, :], block, NT, preferred_element_type=F32
        )

    def send_parts(h):
        for first, last in ((1, 4), (4, 8)):
            for i in range(first, last):
                part_s[h, (t + i) % 8] = input_part(h, (t + i) % 8).astype(BF)
            for i in range(first, last):
                owner(h, i, t, (t + i) % 8).start()
        own_part[h] = input_part(h, t)

    def add_parts(h):
        def body(i, carry):
            sender = (t - i + 8) % 8
            owner(h, i, sender, t).wait_recv()
            own_part[h] += part_r[h, sender].astype(F32)
            return carry

        lax.fori_loop(1, 8, body, 0)
        ig[h, t] = own_part[h].astype(BF)

        def send(i, carry):
            spread(h, i, t).start()
            return carry

        lax.fori_loop(1, 8, send, 0)

    def take_ig(h):
        def body(i, carry):
            spread(h, i, (t - i + 8) % 8).wait_recv()
            return carry

        lax.fori_loop(1, 8, body, 0)

    pass_on(fx[0], hops_x, near)
    pass_across(fx[0])
    pass_on(fx[1], hops_x, far)
    loads[2].wait()
    complete(fx[0])
    lay(0, rows_x, order_x, vx_all, 4)
    send_parts(0)
    pass_across(fx[1])
    complete(fx[1])
    lay(1, rows_x, order_x, vx_all, 4)
    send_parts(1)
    pass_on(fc[0], hops_c, near)
    add_parts(0)
    pass_on(fc[1], hops_c, far)
    pass_across(fc[0])
    add_parts(1)
    pass_across(fc[1])
    complete(fc[0])
    lay(0, rows_c, order_c, vc_all, 14)
    complete(fc[1])
    lay(1, rows_c, order_c, vc_all, 14)
    loads[3].wait()

    def cotangent_part(i, carry):
        block = c_ref[pl.ds(pl.multiple_of(i * 256, 256), 256), :]
        part = lax.dot_general(vc_all[...], block, NT, preferred_element_type=F32)
        cg[i * 2] = part[:, :128]
        cg[i * 2 + 1] = part[:, 128:]
        return carry

    lax.fori_loop(0, 4, cotangent_part, 0)
    terms = []
    for h in range(2):
        take_ig(h)
        terms.append(
            [
                jnp.sum(ig[h, k].astype(F32) * cg[k, h * 128 : (h + 1) * 128], axis=0, keepdims=True)
                for k in range(8)
            ]
        )
    score[t] = jnp.concatenate([a + b for a, b in zip(*terms)], axis=0)

    def share(i, sender):
        return remote(
            score.at[sender], score.at[sender], sc_ss.at[i], sc_rs.at[i], at(t=(t + i) % 8)
        )

    def send_score(i, carry):
        share(i, t).start()
        return carry

    def take_score(i, carry):
        share(i, (t - i + 8) % 8).wait_recv()
        return carry

    lax.fori_loop(1, 8, send_score, 0)
    lax.fori_loop(1, 8, take_score, 0)
    total = score[0]
    for k in range(1, 8):
        total += score[k]
    minus = total * (-1.0 / math.sqrt(D * FF * VAL))
    raw = jnp.maximum(minus, 0.0) + jnp.log1p(jnp.exp(-jnp.abs(minus)))
    for h in range(2):
        for k in range(8):
            exact = ig[h, k].astype(F32) * raw[k : k + 1, :]
            high = exact.astype(BF)
            columns = slice(k * 128, (k + 1) * 128)
            coef[h * 128 : (h + 1) * 128, columns] = high
            coef[256 + h * 128 : 256 + (h + 1) * 128, columns] = (exact - high.astype(F32)).astype(BF)
    mine_raw = jnp.sum(
        jnp.where(lax.broadcasted_iota(jnp.int32, (8, 128), 0) == t, raw, 0.0),
        axis=0,
        keepdims=True,
    )
    tot_s[0] = jnp.broadcast_to(jnp.sum(raw, keepdims=True), (8, 128))

    used = iter(range(64))

    def move(src, dst, device):
        k = next(used)
        return start(remote(src, dst, lk_ss.at[k], lk_rs.at[k], device))

    def cross(n):
        return remote(
            lp.at[n, :, 1], core_r.at[n], co_ss.at[n], co_rs.at[n], at(core=1 - core)
        )

    tot_core = move(tot_s.at[0], tot_r.at[0], at(core=1 - core))

    def look_part(n):
        part = dot(coef[...], c_ref[:, pl.ds(pl.multiple_of(n * 256, 256), 256)])
        lp[n] = (part[:256] + part[256:]).reshape(2, 2, 64, 256)
        cross(n).start()

    def cross_sum(n):
        cross(n).wait_recv()
        part = lp[n, :, 0] + core_r[n]
        columns = pl.ds(pl.multiple_of(n * 256, 256), 256)
        for a in range(2):
            for r in range(4):
                first = (a * 4 + r) * 8
                rows = jnp.concatenate([part[0, first : first + 8], part[1, first : first + 8]], axis=0)
                z1_s[a, r, :, columns] = rows.astype(BF)
                if a == 0 and r == 0:
                    s0[:, columns] = rows

    def send_near(columns, two):
        copies = []
        for a, step, slot in (
            (1, two, 5), (0, two, 6), (1, -1, 3), (1, 1, 1), (0, -1, 4), (0, 1, 2), (1, 0, 0)
        ):
            copies.append(
                move(
                    z1_s.at[a, step % 4, :, columns],
                    z1_r.at[pl.ds(slot * 16, 16), columns],
                    at(z=zed(step), xlo=(xlo + a) % 2),
                )
            )
        return copies

    groups = ((0, 512), (512, 512), (1024, 512), (1536, 256))

    def both(n, carry):
        look_part(n)
        cross_sum(n - 2)
        return carry

    near_sums = []

    def send_group(k):
        first, size = groups[k]
        near_sums.append(send_near(pl.ds(first, size), 2 if first < LEFT else -2))

    look_part(0)
    look_part(1)
    lax.fori_loop(2, 4, both, 0)
    send_group(0)
    lax.fori_loop(4, 6, both, 0)
    send_group(1)
    look_part(6)
    tot_core.wait_recv()
    tot_s[1] = tot_s[0] + tot_r[0]
    tots = []
    for k, (a, step) in enumerate(((1, 2), (0, 2), (1, -1), (1, 1), (0, -1), (0, 1), (1, 0))):
        tots.append(move(tot_s.at[1], tot_r.at[1 + k], at(z=zed(step), xlo=(xlo + a) % 2)))
    cross_sum(4)
    cross_sum(5)
    send_group(2)
    cross_sum(6)
    send_group(3)

    def gather_near(back_two):
        row = lax.broadcasted_iota(jnp.int32, (16, 112), 0)
        column = lax.broadcasted_iota(jnp.int32, (16, 112), 1)
        block, slot = row // 4, column // 16
        one = jnp.where(block == 0, 0, jnp.where(block == 1, 3, block - 1))
        two = jnp.where(block == 0, 1, jnp.where(block == 1, 3, jnp.where(block == 2, 0, 2)))
        source = jnp.where((slot == 3) | (slot == 4), one, block)
        if back_two:
            source = jnp.where(slot >= 5, two, source)
        return jnp.where(column % 16 == source * 4 + row % 4, 1.0, 0.0).astype(BF)

    for copy in near_sums[0] + near_sums[1]:
        copy.wait_recv()
    left_sum = s0[:, :LEFT] + dot(gather_near(False), z1_r[:, :LEFT])
    for copy in near_sums[2] + near_sums[3]:
        copy.wait_recv()
    right_sum = s0[:, LEFT:] + dot(gather_near(True), z1_r[:, LEFT:])
    sums = jnp.concatenate([left_sum, right_sum], axis=1)
    for b in (3, 1, 2, 0):
        rows = sums[b * 4 : (b + 1) * 4]
        z2_s[b] = jnp.concatenate([rows[:, :HALF], rows[:, HALF:]], axis=0)
    away = [move(z2_s.at[b], z2_r.at[b], at(z=zed(BLOCKS[b]))) for b in (3, 1, 2)]
    total = tot_s[1]
    for k, copy in enumerate(tots):
        copy.wait_recv()
        total += tot_r[1 + k]
    tot_s[2] = total
    for b in (3, 1, 2):
        away.append(move(tot_s.at[2], tot_r.at[7 + b], at(z=zed(BLOCKS[b]))))
    early = len(pending) - 6
    for copy in pending[:early]:
        copy.wait_send()

    def drain_t(i, carry):
        for h in range(2):
            owner(h, i, t, (t + i) % 8).wait_send()
            spread(h, i, t).wait_send()
        share(i, t).wait_send()
        return carry

    lax.fori_loop(1, 8, drain_t, 0)

    def drain_core(n, carry):
        cross(n).wait_send()
        return carry

    lax.fori_loop(0, 7, drain_core, 0)

    for copy in away:
        copy.wait_recv()
    token_total = tot_s[2] + tot_r[8] + tot_r[9] + tot_r[10]
    whole = z2_s[0] + z2_r[1] + z2_r[2] + z2_r[3]
    out = jnp.concatenate([whole[0:4], whole[4:8]], axis=1) / token_total[0:1, 0:1]
    look_ref[...] = out.astype(BF)
    weights_ref[...] = mine_raw * (TOKENS / token_total[0:1, :])
    for copy in pending[early:]:
        copy.wait_send()


def on_device(train_inputs, train_cotangents, val_inputs, val_cotangents):
    vmem = pl.BlockSpec(memory_space=pltpu.VMEM)
    hbm = pl.BlockSpec(memory_space=pl.ANY)
    dma = pltpu.SemaphoreType.DMA
    weights, look = pl.pallas_call(
        kernel,
        out_shape=(jax.ShapeDtypeStruct((1, 128), F32), jax.ShapeDtypeStruct((4, 1792), BF)),
        in_specs=[hbm] * 4,
        out_specs=(vmem, vmem),
        scratch_shapes=[
            pltpu.VMEM((4, 2304), BF),
            pltpu.VMEM((1024, 512), BF),
            pltpu.VMEM((1024, 1792), BF),
            pltpu.VMEM((2, 2, 2, 8, 80, 128), BF),
            pltpu.VMEM((256, 512), BF),
            pltpu.VMEM((256, 1792), BF),
            pltpu.VMEM((2, 8, 128, 128), BF),
            pltpu.VMEM((2, 8, 128, 128), BF),
            pltpu.VMEM((2, 128, 128), F32),
            pltpu.VMEM((2, 8, 128, 128), BF),
            pltpu.VMEM((8, 256, 128), F32),
            pltpu.VMEM((8, 8, 128), F32),
            pltpu.VMEM((512, 1024), BF),
            pltpu.VMEM((7, 2, 2, 64, 256), F32),
            pltpu.VMEM((7, 2, 64, 256), F32),
            pltpu.VMEM((16, 1792), F32),
            pltpu.VMEM((2, 4, 16, 1792), BF),
            pltpu.VMEM((112, 1792), BF),
            pltpu.VMEM((4, 8, HALF), F32),
            pltpu.VMEM((4, 8, HALF), F32),
            pltpu.VMEM((3, 8, 128), F32),
            pltpu.VMEM((11, 8, 128), F32),
            dma((4,)),
            dma((16,)),
            dma((16,)),
            dma((16,)),
            dma((16,)),
            dma((12,)),
            dma((12,)),
            dma((2, 8)),
            dma((2, 8)),
            dma((2, 8)),
            dma((2, 8)),
            dma((8,)),
            dma((8,)),
            dma((7,)),
            dma((7,)),
            dma((64,)),
            dma((64,)),
        ],
        compiler_params=pltpu.CompilerParams(
            collective_id=0, has_side_effects=True, vmem_limit_bytes=60 << 20
        ),
        name="reweight",
    )(val_inputs, val_cotangents, train_inputs, train_cotangents)
    return weights.reshape(128), look


def solution(mesh):
    return jax.shard_map(
        on_device,
        mesh=mesh,
        in_specs=(P("dp", "tensor"), P("dp", "tensor"), P("dp", "tensor"), P("dp", "tensor")),
        out_specs=(P(("dp", "tensor")), P("dp", "tensor")),
        check_vma=False,
    )
```
